256 devices in a mesh: section: 4 (over x), dp: 4 (over z_hi), tensor: 16 (over y, z_lo, core).
Axes of the slice: x: 4, y: 4, z: 8 (z_hi: 4, z_lo: 2; z = z_hi * 2 + z_lo), core: 2. Of those that a mesh axis runs over, the one named last changes fastest.
Arguments:
- act_input: bfloat16 [4, 2048, 14336], P('section', 'tensor', 'dp'), may hold values from -400 to 400
- ln_gain: float32 [4, 14336], P('section', 'dp'), may hold values from 0.1 to 1.9
- ln_shift: float32 [4, 14336], P('section', 'dp'), may hold values from -3 to 3
- w_proj: bfloat16 [4, 14336, 14336], P('section', 'dp', 'tensor'), may hold values from -0.046875 to 0.046875
- b_proj: float32 [4, 14336], P('section', 'tensor'), may hold values from -3 to 3
- act_ids: int32 [2048], P('dp'), may hold values from 0 to 127
- sent_copy: bfloat16 [4, 512, 14336], P('section', 'dp', 'tensor'), may hold values from -64 to 64
- held_copy: bfloat16 [4, 512, 14336], P('section', 'dp', 'tensor'), may hold values from -6 to 6
- grad_input: bfloat16 [4, 2048, 14336], P('section', 'tensor', 'dp'), may hold values from -6 to 6
- grad_ids: int32 [2048], P('tensor'), may hold values from 0 to 127
- back_sent: bfloat16 [4, 2048, 14336], P('section', 'tensor', 'dp'), may hold values from -64 to 64
- back_held: bfloat16 [4, 2048, 14336], P('section', 'tensor', 'dp'), may hold values from -6 to 6
Outputs:
- arrived: bfloat16 [4, 2048, 14336], P('section', 'dp', 'tensor')
- grad_arrived: bfloat16 [4, 2048, 14336], P('section', 'tensor', 'dp')
The draws below stay inside these ranges and needn't reach their ends.
Inputs may be any that keep to these rules, and one draw needn't show every extreme that they name: `act_ids`: a slot within the block of 128 activation store rows of the token's data group. `grad_ids`: a slot within the block of 128 gradient store rows of the token's block of 128 tokens.
All inputs are finite; a program needn't handle non-finite values.
Results may differ from the reference program's by a relative error of at most 0.015.
Values may be sent and summed in bfloat16 or wider, within the bound.
A program may use at most 128 MiB of HBM per device.

```python
import math
import jax
import jax.numpy as jnp
from jax import lax

D = 14336
HB = 128
TOK_DEV = 512
SLOT_DEV = 128
SECTIONS = 4
TOKENS = 2048
TENSOR_ROWS = 128
SLOTS_A = 512
SLOTS_G = 2048


def draw_act_input(key, part):
    key = jax.random.fold_in(key, 11)
    base_key, column_key, row_key = jax.random.split(key, 3)
    ramp = jnp.arange(D, dtype=jnp.float32) / (D - 1)
    column_scale = jnp.exp(0.5 * math.log(10.0) * (ramp + jax.random.uniform(column_key, (D,), jnp.float32)))
    base = jax.random.truncated_normal(base_key, -4.0, 4.0, (SECTIONS, TOKENS, D), jnp.float32)
    row_scale = jnp.exp(math.log(10.0) * jax.random.uniform(row_key, (SECTIONS, TOKENS, 1), jnp.float32))
    return (base * row_scale * column_scale).astype(jnp.bfloat16)


def outlier_store(key, rows, low, high):
    base_key, pick_key, size_key = jax.random.split(key, 3)
    base = jax.random.truncated_normal(base_key, -4.0, 4.0, (SECTIONS, rows, D), jnp.float32)
    picked = jax.random.uniform(pick_key, (SECTIONS, 1, D), jnp.float32) < 1.0 / 32.0
    sizes = jnp.exp(math.log(low) + (math.log(high) - math.log(low)) * jax.random.uniform(size_key, (SECTIONS, 1, D), jnp.float32))
    column_scale = jnp.where(picked, sizes, 1.0)
    return (base * column_scale).astype(jnp.bfloat16)


def draw_sent_copy(key, part):
    key = jax.random.fold_in(key, 23)
    return outlier_store(key, SLOTS_A, 4.0, 12.0)


def draw_back_sent(key, part):
    key = jax.random.fold_in(key, 37)
    return outlier_store(key, SLOTS_G, 4.0, 12.0)


def with_ends(array, stream_key, low, high):
    longest = array.shape.index(max(array.shape))
    spots = []
    for shift in (0, 1):
        where = [jax.random.randint(jax.random.fold_in(stream_key, axis), (), 0, length) for axis, length in enumerate(array.shape)]
        where[longest] = (where[longest] + shift) % array.shape[longest]
        spots.append(tuple(where))
    return array.at[spots[0]].set(low).at[spots[1]].set(high)


def shard_levels(key, shape, cuts, low, top_value):
    factor_of = 1.0
    for dim, shards_of in cuts:
        draws = jax.random.uniform(jax.random.fold_in(jax.random.fold_in(key, 6), dim), (shards_of,), jnp.float32, low / len(cuts), top_value / len(cuts))
        factor_of = factor_of * jnp.repeat(jnp.exp(draws), shape[dim] // shards_of).reshape((-1,) + (1,) * (len(shape) - 1 - dim))
    return factor_of


def bell_draw(key, extent, width, most, pieces=(), kind=jnp.bfloat16):
    drawn = jax.random.normal(key, extent, jnp.float32) * width
    if len(pieces) > 0:
        drawn = shard_levels(key, extent, pieces, -0.22, 0.18) * drawn
    return jnp.clip(drawn, min=-most, max=most).astype(kind)


def setup_inputs(seed: int = 0) -> dict:
    seeds = jax.random.split(jax.random.key(seed), 13)
    return {
        "act_input": draw_act_input(jax.random.fold_in(seeds[12], 71), 0),
        "ln_gain": jnp.clip(1.0 + 0.18 * jax.random.normal(seeds[1], (SECTIONS, D), jnp.float32), 0.1, 1.9),
        "ln_shift": bell_draw(seeds[2], (SECTIONS, D), 0.5, 3.0, ((0, 4), (1, 4)), jnp.float32),
        "w_proj": bell_draw(seeds[3], (SECTIONS, D, D), D ** -0.5, 0.046875, ((0, 4), (1, 4), (2, 16))),
        "b_proj": bell_draw(seeds[4], (SECTIONS, D), 0.5, 3.0, ((0, 4), (1, 16)), jnp.float32),
        "act_ids": with_ends(jax.random.randint(seeds[5], (TOKENS,), 0, SLOT_DEV), jax.random.fold_in(seeds[5], 1), 0, SLOT_DEV - 1).astype(jnp.int32),
        "sent_copy": draw_sent_copy(jax.random.fold_in(seeds[12], 71), 0),
        "held_copy": bell_draw(seeds[7], (SECTIONS, SLOTS_A, D), 1.0, 6.0, ((0, 4), (1, 4), (2, 16))),
        "grad_input": bell_draw(seeds[8], (SECTIONS, TOKENS, D), 1.0, 6.0, ((0, 4), (1, 16), (2, 4))),
        "grad_ids": with_ends(jax.random.randint(seeds[9], (TOKENS,), 0, SLOT_DEV), jax.random.fold_in(seeds[9], 1), 0, SLOT_DEV - 1).astype(jnp.int32),
        "back_sent": draw_back_sent(jax.random.fold_in(seeds[12], 71), 0),
        "back_held": bell_draw(seeds[11], (SECTIONS, SLOTS_G, D), 1.0, 6.0, ((0, 4), (1, 16), (2, 4))),
    }


epsilon = 1e-05
scale_epsilon = 1e-06
clip_level = 2.5

def hadamard_table(order):
    index = jnp.arange(order, dtype=jnp.int32)
    common = jnp.bitwise_and(index[:, None], index[None, :])
    parity = jnp.zeros_like(common)
    for bit in range(order.bit_length()):
        parity = parity + jnp.bitwise_and(jnp.right_shift(common, bit), 1)
    signs = 1.0 - 2.0 * jnp.remainder(parity, 2).astype(jnp.float32)
    return (signs / math.sqrt(order)).astype(jnp.float32)

def rotate(values):
    table = hadamard_table(HB)
    leading = values.shape[0]
    blocks = values.reshape(leading, -1, HB)
    turned = jnp.einsum('rbk,kl->rbl', blocks, table, precision=lax.Precision.HIGHEST)
    return turned.reshape(values.shape)

def encode(delta):
    leading = delta.shape[0]
    turned = rotate(delta).reshape(leading, -1, HB)
    block_scale = jnp.sqrt(lax.optimization_barrier(jnp.mean(turned * turned, axis=2)) + scale_epsilon).astype(jnp.bfloat16)
    levels = jnp.clip(turned / block_scale.astype(jnp.float32)[:, :, None], -clip_level, clip_level)
    return (levels.astype(jnp.bfloat16).reshape(delta.shape), block_scale)

def decode(held_rows, coded, block_scale):
    leading = coded.shape[0]
    spread = coded.astype(jnp.float32).reshape(leading, -1, HB) * block_scale.astype(jnp.float32)[:, :, None]
    return (held_rows.astype(jnp.float32) + rotate(spread.reshape(coded.shape))).astype(jnp.bfloat16)

def reference(act_input, ln_gain, ln_shift, w_proj, b_proj, act_ids, sent_copy, held_copy, grad_input, grad_ids, back_sent, back_held):
    positions = jnp.arange(TOKENS, dtype=jnp.int32)
    act_rows = positions // TOK_DEV * SLOT_DEV + act_ids
    grad_rows = positions // TENSOR_ROWS * SLOT_DEV + grad_ids
    arrived_list = [None] * SECTIONS
    grad_list = [None] * SECTIONS
    for section in range(SECTIONS):
        values = act_input[section].astype(jnp.float32)
        row_mean = lax.optimization_barrier(jnp.sum(values, axis=1)) / D
        row_var = lax.optimization_barrier(jnp.sum(values * values, axis=1)) / D - row_mean * row_mean
        normed = ((values - row_mean[:, None]) * lax.rsqrt(row_var + epsilon)[:, None] * ln_gain[section] + ln_shift[section]).astype(jnp.bfloat16)
        output = jnp.dot(normed, w_proj[section], preferred_element_type=jnp.float32) + b_proj[section]
        delta = output - sent_copy[section][act_rows].astype(jnp.float32)
        coded, block_scale = encode(delta)
        target = (section + 1) % SECTIONS
        arrived_list[target] = decode(held_copy[target][act_rows], coded, block_scale)
        grad_delta = grad_input[section].astype(jnp.float32) - back_sent[section][grad_rows].astype(jnp.float32)
        grad_coded, grad_scale = encode(grad_delta)
        source = (section - 1) % SECTIONS
        grad_list[source] = decode(back_held[source][grad_rows], grad_coded, grad_scale)
    return (jnp.stack(arrived_list), jnp.stack(grad_list))
```

```python
import functools
import math

import jax
import jax.numpy as jnp
from jax import lax
from jax.experimental import pallas as pl
from jax.experimental.pallas import tpu as pltpu
from jax.sharding import PartitionSpec as P

D = 14336
HB = 128
KD = 3584
ND = 896
TR = 128
PIECES = 8
PR = TR // PIECES
PLANE = 8 * PR
GB = 4
GSTEPS = KD // (HB * GB)
GC = GB * HB

epsilon = 1e-05
scale_epsilon = 1e-06
clip_level = 2.5

MESH = pl.DeviceIdType.MESH
f32 = jnp.float32
bf16 = jnp.bfloat16


def dot(a, b):
    return jnp.dot(a, b, preferred_element_type=f32)


def clipped(tu):
    mean = jnp.sum(tu * tu, axis=1, keepdims=True) * (1.0 / (HB * HB))
    scale = jnp.sqrt(mean + scale_epsilon).astype(bf16).astype(f32)
    bound = scale * (clip_level / math.sqrt(HB))
    return jnp.clip(tu * (1.0 / HB), -bound, bound).astype(bf16)


def kernel(
    x_hbm, gain, shift, w_hbm, bias, aids, sent_hbm, held_hbm, gi_hbm, gids, bs_hbm, bh_hbm,
    out_hbm, gout_hbm,
    xin, w, sent, held, gi, bs, bh, xg, pbuf, m1, m2, wout, win, obuf, gwout, gwin, gobuf,
    table, oha, ohg, st_out, st_in, mean_l, rstd_l,
    lsem, osem, gosem, ag_s, ag_r, m1_s, m1_r, m2_s, m2_r, wr_s, wr_r, gw_s, gw_r, st_s, st_r,
):
    s = lax.axis_index("section")
    d = lax.axis_index("dp")
    t = lax.axis_index("tensor")
    y = t // 4
    zl = (t // 2) % 2
    c = t % 2
    yn, yp = (y + 1) % 4, (y + 3) % 4
    y2 = (y + 2) % 4

    def dev(ds=0, dd=0, y_=None, zl_=None, c_=None):
        y_ = y if y_ is None else y_
        zl_ = zl if zl_ is None else zl_
        c_ = c if c_ is None else c_
        return ((s + ds) % 4, (d + dd) % 4, y_ * 4 + zl_ * 2 + c_)

    z_peer = dev(zl_=1 - zl)
    y_next, y_prev = dev(y_=yn), dev(y_=yp)
    sibling = dev(c_=1 - c)

    loads = [
        pltpu.make_async_copy(a, b, lsem.at[i])
        for i, (a, b) in enumerate(
            (
                (x_hbm, xin), (gi_hbm, gi), (bs_hbm, bs), (w_hbm, w),
                (sent_hbm, sent), (held_hbm, held), (bh_hbm, bh),
            )
        )
    ]
    for load in loads:
        load.start()

    barrier = pltpu.get_barrier_semaphore()
    peers = [z_peer, y_next, y_prev, sibling, dev(dd=1), dev(dd=2), dev(dd=3), dev(ds=1), dev(ds=3)]
    for peer in peers:
        pl.semaphore_signal(barrier, inc=1, device_id=peer, device_id_type=MESH)

    row = lax.broadcasted_iota(jnp.int32, (HB, HB), 0)
    lane = lax.broadcasted_iota(jnp.int32, (HB, HB), 1)
    both = row & lane
    both = both ^ (both >> 4)
    both = both ^ (both >> 2)
    both = both ^ (both >> 1)
    signs = (1 - 2 * (both & 1)).astype(f32)
    table[0:HB] = signs.astype(bf16)
    table[HB : 2 * HB] = signs.astype(bf16)
    table[2 * HB : 3 * HB] = (-signs).astype(bf16)
    lane_f = lane.astype(f32)

    def picked(ids_row):
        column = jnp.transpose(jnp.broadcast_to(ids_row.astype(f32), (HB, HB)))
        return jnp.where(column == lane_f, 1.0, 0.0).astype(bf16)

    for q in range(4):
        oha[q] = picked(aids[q : q + 1, :])
    ohg[...] = picked(gids[0:1, :])

    loads[0].wait()

    def stat(i, carry):
        rows = pl.ds(pl.multiple_of(i * 16, 16), 16)
        v = xin[rows, :].astype(f32)
        mean_l[rows, :] = jnp.broadcast_to(jnp.sum(v, axis=1, keepdims=True), (16, HB))
        rstd_l[rows, :] = jnp.broadcast_to(jnp.sum(v * v, axis=1, keepdims=True), (16, HB))
        return carry

    lax.fori_loop(0, TR // 16, stat, 0)
    packed = jnp.where(lane == 0, mean_l[...], rstd_l[...])
    st_out[...] = jnp.transpose(packed)[0:8, :]
    pl.semaphore_wait(barrier, len(peers))

    def st_copy(j):
        return pltpu.make_async_remote_copy(
            src_ref=st_out, dst_ref=st_in.at[j], send_sem=st_s.at[j], recv_sem=st_r.at[j],
            device_id=dev(dd=j + 1), device_id_type=MESH,
        )

    for j in range(3):
        st_copy(j).start()
    for j in range(3):
        st_copy(j).wait_recv()
    total = st_out[...] + st_in[0] + st_in[1] + st_in[2]
    mean = total[0:1, :] * (1.0 / D)
    var = total[1:2, :] * (1.0 / D) - mean * mean
    rstd = lax.rsqrt(var + epsilon)
    mean_l[...] = jnp.transpose(jnp.broadcast_to(mean, (HB, HB)))
    rstd_l[...] = jnp.transpose(jnp.broadcast_to(rstd, (HB, HB)))

    def slot(c_, y_, zl_):
        return pl.ds(pl.multiple_of(c_ * PLANE + y_ * (2 * PR) + zl_ * PR, PR), PR)

    def group(c_, y_):
        return pl.ds(pl.multiple_of(c_ * PLANE + y_ * (2 * PR), 2 * PR), 2 * PR)

    sends = (
        (slot(c, y, zl), z_peer),
        (slot(c, y, zl), y_next),
        (slot(c, y, zl), y_prev),
        (slot(c, y, 1 - zl), y_next),
        (slot(c, y, 1 - zl), y_prev),
        (slot(c, yp, 1), y_next),
        (slot(c, yn, 0), y_prev),
        (group(c, y), sibling),
        (group(c, yp), sibling),
        (group(c, yn), sibling),
        (group(c, y2), sibling),
    )
    comes = (
        slot(c, y, 1 - zl),
        slot(c, yp, zl),
        slot(c, yn, zl),
        slot(c, yp, 1 - zl),
        slot(c, yn, 1 - zl),
        slot(c, y2, 1),
        slot(c, y2, 0),
        group(1 - c, y),
        group(1 - c, yp),
        group(1 - c, yn),
        group(1 - c, y2),
    )

    def ag(kind, p):
        rows, peer = sends[kind]
        return pltpu.make_async_remote_copy(
            src_ref=xg.at[p, rows], dst_ref=xg.at[p, rows],
            send_sem=ag_s.at[p, kind], recv_sem=ag_r.at[p, kind],
            device_id=peer, device_id_type=MESH,
        )

    def ag_wait(kind, p):
        rows, peer = comes[kind], sends[kind][1]
        pltpu.make_async_remote_copy(
            src_ref=xg.at[p, rows], dst_ref=xg.at[p, rows],
            send_sem=ag_s.at[p, kind], recv_sem=ag_r.at[p, kind],
            device_id=peer, device_id_type=MESH,
        ).wait_recv()

    def half(h, dest):
        return pl.ds(pl.multiple_of(h * PLANE + dest * (2 * PR), 2 * PR), 2 * PR)

    dn, dq, d2 = (d + 1) % 4, (d + 3) % 4, (d + 2) % 4

    def first(way, p):
        return pltpu.make_async_remote_copy(
            src_ref=pbuf.at[p, half(1 - way, d2)], dst_ref=m1.at[p, way],
            send_sem=m1_s.at[p, way], recv_sem=m1_r.at[p, way],
            device_id=dev(dd=1 if way == 0 else 3), device_id_type=MESH,
        )

    def second(way, h, p):
        return pltpu.make_async_remote_copy(
            src_ref=pbuf.at[p, half(h, dn if way == 0 else dq)], dst_ref=m2.at[p, way, h],
            send_sem=m2_s.at[p, way, h], recv_sem=m2_r.at[p, way, h],
            device_id=dev(dd=1 if way == 0 else 3), device_id_type=MESH,
        )

    def wire(p):
        return pltpu.make_async_remote_copy(
            src_ref=wout.at[p], dst_ref=win.at[p], send_sem=wr_s.at[p], recv_sem=wr_r.at[p],
            device_id=dev(ds=1), device_id_type=MESH,
        )

    def grad_wire(g):
        return pltpu.make_async_remote_copy(
            src_ref=gwout.at[g], dst_ref=gwin.at[g], send_sem=gw_s.at[g], recv_sem=gw_r.at[g],
            device_id=dev(ds=3), device_id_type=MESH,
        )

    def out_copy(p):
        rows = pl.ds(pl.multiple_of(p * PR, PR), PR)
        return pltpu.make_async_copy(obuf.at[:, rows], out_hbm.at[:, rows], osem.at[p])

    def gout_copy(g):
        columns = pl.ds(pl.multiple_of(g * GC, GC), GC)
        return pltpu.make_async_copy(gobuf.at[:, columns], gout_hbm.at[:, columns], gosem.at[g])

    def own_rows(p):
        rows = pl.ds(pl.multiple_of(p * PR, PR), PR)
        return jnp.concatenate([oha[0, rows], oha[2, rows], oha[1, rows], oha[3, rows]], axis=0)

    def stage_own(p):
        rows = pl.ds(pl.multiple_of(p * PR, PR), PR)
        v = xin[rows, :].astype(f32)
        v = (v - mean_l[rows, 0:1]) * rstd_l[rows, 0:1] * gain[...] + shift[...]
        xg[p, slot(c, y, zl), :] = v.astype(bf16)
        for kind in (0, 1, 2):
            ag(kind, p).start()

    def stage_near(p):
        ag_wait(0, p)
        ag(3, p).start()
        ag(4, p).start()
        ag(7, p).start()
        ag_wait(1, p)
        ag_wait(2, p)

        @pl.when(zl == 1)
        def _():
            ag(5, p).start()

        @pl.when(zl == 0)
        def _():
            ag(6, p).start()

    def stage_far(p):
        ag_wait(3, p)
        ag_wait(4, p)

        @pl.when(zl == 0)
        def _():
            ag(5, p).start()

        @pl.when(zl == 1)
        def _():
            ag(6, p).start()

        ag(8, p).start()
        ag(9, p).start()

    def stage_opposite(p):
        ag_wait(5, p)
        ag_wait(6, p)
        ag(10, p).start()

    def stage_product(p):
        for kind in (7, 8, 9, 10):
            ag_wait(kind, p)
        pbuf[p] = dot(xg[p], w[...]).astype(bf16)
        first(0, p).start()
        first(1, p).start()
        second(0, 0, p).start()
        second(1, 1, p).start()

    def stage_sum(p):
        for way in (0, 1):
            first(way, p).wait_recv()
            rows = half(1 - way, dn if way == 0 else dq)
            pbuf[p, rows, :] = (pbuf[p, rows, :].astype(f32) + m1[p, way].astype(f32)).astype(bf16)
            second(way, 1 - way, p).start()

    def stage_code(p):
        for way in (0, 1):
            for h in (0, 1):
                second(way, h, p).wait_recv()
        parts = []
        for h in (0, 1):
            parts.append(
                pbuf[p, half(h, d), :].astype(f32) + m2[p, 0, h].astype(f32) + m2[p, 1, h].astype(f32)
            )
        delta = jnp.concatenate(parts, axis=0) + bias[...] - dot(own_rows(p), sent[...])
        for b in range(ND // HB):
            columns = slice(b * HB, (b + 1) * HB)
            high = delta[:, columns].astype(bf16)
            low = (delta[:, columns] - high.astype(f32)).astype(bf16)
            tu = dot(jnp.concatenate([high, low], axis=1), table[0 : 2 * HB])
            wout[p, :, columns] = clipped(tu)
        wire(p).start()

    def stage_decode(p):
        wire(p).wait_recv()
        chosen = own_rows(p)
        rows = pl.ds(pl.multiple_of(p * PR, PR), PR)
        for b in range(ND // HB):
            columns = slice(b * HB, (b + 1) * HB)
            value = dot(
                jnp.concatenate([chosen, win[p, :, columns]], axis=1),
                jnp.concatenate([held[:, columns], table[0:HB]], axis=0),
            ).astype(bf16)
            for i, q in enumerate((0, 2, 1, 3)):
                obuf[q, rows, columns] = value[i * PR : (i + 1) * PR]
        out_copy(p).start()

    def stage_grad(g):
        for b in range(GB):
            columns = pl.ds(pl.multiple_of(g * GC + b * HB, HB), HB)
            stored = dot(ohg[...], bs[:, columns]).astype(bf16)
            tu = dot(jnp.concatenate([gi[:, columns], stored], axis=1), table[HB : 3 * HB])
            gwout[g, :, b * HB : (b + 1) * HB] = clipped(tu)
        grad_wire(g).start()

    def stage_grad_decode(g):
        grad_wire(g).wait_recv()
        for b in range(GB):
            columns = pl.ds(pl.multiple_of(g * GC + b * HB, HB), HB)
            gobuf[:, columns] = dot(
                jnp.concatenate([ohg[...], gwin[g, :, b * HB : (b + 1) * HB]], axis=1),
                jnp.concatenate([bh[:, columns], table[0:HB]], axis=0),
            ).astype(bf16)
        gout_copy(g).start()

    def at(k, delay, stage, count=PIECES):
        p = k - delay

        @pl.when((p >= 0) & (p < count))
        def _():
            stage(p)

    def tick(k, carry):
        at(k, 0, stage_own)
        at(k, 1, stage_near)
        at(k, 2, stage_far)
        at(k, 3, stage_opposite)

        @pl.when(k == 0)
        def _():
            loads[1].wait()
            loads[2].wait()

        @pl.when(k == 4)
        def _():
            for i in (3, 4, 5, 6):
                loads[i].wait()

        at(k, 4, stage_product)
        at(k, 5, stage_sum)
        at(k, 6, stage_code)
        at(k, 7, stage_decode)
        at(k, 0, stage_grad, GSTEPS)
        at(k, 5, stage_grad_decode, GSTEPS)
        return carry

    lax.fori_loop(0, PIECES + 7, tick, 0)

    for j in range(3):
        st_copy(j).wait_send()

    def finish(p, carry):
        for kind in range(11):
            ag(kind, p).wait_send()
        for way in (0, 1):
            first(way, p).wait_send()
            for h in (0, 1):
                second(way, h, p).wait_send()
        wire(p).wait_send()
        out_copy(p).wait()
        return carry

    lax.fori_loop(0, PIECES, finish, 0)

    def finish_grad(g, carry):
        grad_wire(g).wait_send()
        gout_copy(g).wait()
        return carry

    lax.fori_loop(0, GSTEPS, finish_grad, 0)


def shards(
    act_input, ln_gain, ln_shift, w_proj, b_proj, act_ids, sent_copy, held_copy,
    grad_input, grad_ids, back_sent, back_held,
):
    anywhere = pl.BlockSpec(memory_space=pl.ANY)
    vmem = pl.BlockSpec(memory_space=pltpu.VMEM)
    dma = pltpu.SemaphoreType.DMA
    arrived, grad_arrived = pl.pallas_call(
        kernel,
        out_shape=(
            jax.ShapeDtypeStruct((4, TR, ND), bf16),
            jax.ShapeDtypeStruct((TR, KD), bf16),
        ),
        in_specs=[
            anywhere, vmem, vmem, anywhere, vmem, vmem, anywhere, anywhere, anywhere, vmem, anywhere, anywhere,
        ],
        out_specs=(anywhere, anywhere),
        scratch_shapes=[
            pltpu.VMEM((TR, KD), bf16),
            pltpu.VMEM((KD, ND), bf16),
            pltpu.VMEM((HB, ND), bf16),
            pltpu.VMEM((HB, ND), bf16),
            pltpu.VMEM((TR, KD), bf16),
            pltpu.VMEM((HB, KD), bf16),
            pltpu.VMEM((HB, KD), bf16),
            pltpu.VMEM((PIECES, 2 * PLANE, KD), bf16),
            pltpu.VMEM((PIECES, 2 * PLANE, ND), bf16),
            pltpu.VMEM((PIECES, 2, 2 * PR, ND), bf16),
            pltpu.VMEM((PIECES, 2, 2, 2 * PR, ND), bf16),
            pltpu.VMEM((PIECES, 4 * PR, ND), bf16),
            pltpu.VMEM((PIECES, 4 * PR, ND), bf16),
            pltpu.VMEM((4, TR, ND), bf16),
            pltpu.VMEM((GSTEPS, TR, GC), bf16),
            pltpu.VMEM((GSTEPS, TR, GC), bf16),
            pltpu.VMEM((TR, KD), bf16),
            pltpu.VMEM((3 * HB, HB), bf16),
            pltpu.VMEM((4, TR, HB), bf16),
            pltpu.VMEM((TR, HB), bf16),
            pltpu.VMEM((8, HB), f32),
            pltpu.VMEM((3, 8, HB), f32),
            pltpu.VMEM((TR, HB), f32),
            pltpu.VMEM((TR, HB), f32),
            dma((7,)),
            dma((PIECES,)),
            dma((GSTEPS,)),
            dma((PIECES, 11)),
            dma((PIECES, 11)),
            dma((PIECES, 2)),
            dma((PIECES, 2)),
            dma((PIECES, 2, 2)),
            dma((PIECES, 2, 2)),
            dma((PIECES,)),
            dma((PIECES,)),
            dma((GSTEPS,)),
            dma((GSTEPS,)),
            dma((3,)),
            dma((3,)),
        ],
        compiler_params=pltpu.CompilerParams(
            collective_id=0, has_side_effects=True, vmem_limit_bytes=56 * 2**20
        ),
        cost_estimate=pl.CostEstimate(
            flops=2 * 2048 * KD * ND, bytes_accessed=14 * 2**20, transcendentals=0
        ),
        name="relay",
    )(
        act_input[0], ln_gain, ln_shift, w_proj[0], b_proj, act_ids.reshape(4, TR),
        sent_copy[0], held_copy[0], grad_input[0], grad_ids.reshape(1, TR), back_sent[0], back_held[0],
    )
    return (arrived.reshape(1, 4 * TR, ND), grad_arrived[None])


def solution(mesh):
    placed = (
        P("section", "tensor", "dp"),
        P("section", "dp"),
        P("section", "dp"),
        P("section", "dp", "tensor"),
        P("section", "tensor"),
        P("dp"),
        P("section", "dp", "tensor"),
        P("section", "dp", "tensor"),
        P("section", "tensor", "dp"),
        P("tensor"),
        P("section", "tensor", "dp"),
        P("section", "tensor", "dp"),
    )
    return jax.shard_map(
        shards,
        mesh=mesh,
        in_specs=placed,
        out_specs=(P("section", "dp", "tensor"), P("section", "tensor", "dp")),
        check_vma=False,
    )
```

```python
import functools
import math

import jax
import jax.numpy as jnp
from jax import lax
from jax.experimental import pallas as pl
from jax.experimental.pallas import tpu as pltpu
from jax.sharding import PartitionSpec as P

D = 14336
HB = 128
KD = 3584
ND = 896
TR = 128
PIECES = 8
PR = TR // PIECES
PLANE = 8 * PR
GB = 4
GSTEPS = KD // (HB * GB)
GC = GB * HB
AHEAD = 2
CODE_DELAY = 4
GRAD_DELAY = 1
PARTS = ((0, 512), (512, 384))

epsilon = 1e-05
scale_epsilon = 1e-06
clip_level = 2.5

MESH = pl.DeviceIdType.MESH
f32 = jnp.float32
bf16 = jnp.bfloat16


def dot(a, b):
    return jnp.dot(a, b, preferred_element_type=f32)


def clipped(tu):
    mean = jnp.sum(tu * tu, axis=1, keepdims=True) * (1.0 / (HB * HB))
    scale = jnp.sqrt(mean + scale_epsilon).astype(bf16).astype(f32)
    bound = scale * (clip_level / math.sqrt(HB))
    return jnp.clip(tu * (1.0 / HB), -bound, bound).astype(bf16)


def kernel(
    x_hbm, gain_hbm, shift_hbm, w_hbm, bias_hbm, aids_hbm, sent_hbm, held_hbm, gi_hbm, gids_hbm, bs_hbm, bh_hbm,
    obuf, gobuf,
    xin, gain, shift, bias, aids, gids, w, sent, held, gi, bs, bh, xr, xg, pbuf, m1, m2, wout, win, gwout, gwin,
    table, oha, ohg, st_out, st_in, tok_out, tok_in, stat_t,
    lsem, ag_s, ag_r, m1_s, m1_r, m2_s, m2_r, wr_s, wr_r, gw_s, gw_r, st_s, st_r, tok_s, tok_r,
):
    s = lax.axis_index("section")
    d = lax.axis_index("dp")
    t = lax.axis_index("tensor")
    y = t // 4
    zl = (t // 2) % 2
    c = t % 2
    yn, yp = (y + 1) % 4, (y + 3) % 4
    y2 = (y + 2) % 4

    def dev(ds=0, dd=0, y_=None, zl_=None, c_=None):
        y_ = y if y_ is None else y_
        zl_ = zl if zl_ is None else zl_
        c_ = c if c_ is None else c_
        return ((s + ds) % 4, (d + dd) % 4, y_ * 4 + zl_ * 2 + c_)

    z_peer = dev(zl_=1 - zl)
    y_next, y_prev = dev(y_=yn), dev(y_=yp)
    sibling = dev(c_=1 - c)

    loads = [
        pltpu.make_async_copy(a, b, lsem.at[i])
        for i, (a, b) in enumerate(
            (
                (x_hbm, xin), (aids_hbm, aids), (gids_hbm, gids), (gain_hbm, gain), (shift_hbm, shift), (bias_hbm, bias),
                (gi_hbm, gi), (bs_hbm, bs), (w_hbm, w), (sent_hbm, sent), (held_hbm, held), (bh_hbm, bh),
            )
        )
    ]
    barrier = pltpu.get_barrier_semaphore()
    plane = [(0, 1), (1, 0), (3, 0), (1, 1), (3, 1), (2, 0), (2, 1)]
    plane_peers = [dev(y_=(y + a) % 4, zl_=(zl + b) % 2) for a, b in plane]
    peers = plane_peers + [sibling, dev(dd=1), dev(dd=2), dev(dd=3), dev(ds=1), dev(ds=3)]
    for peer in peers:
        pl.semaphore_signal(barrier, inc=1, device_id=peer, device_id_type=MESH)
    for load in loads[0:6]:
        load.start()

    row = lax.broadcasted_iota(jnp.int32, (HB, HB), 0)
    lane = lax.broadcasted_iota(jnp.int32, (HB, HB), 1)
    both = row & lane
    both = both ^ (both >> 4)
    both = both ^ (both >> 2)
    both = both ^ (both >> 1)
    signs = (1 - 2 * (both & 1)).astype(f32)
    table[0:HB] = signs.astype(bf16)
    table[HB : 2 * HB] = signs.astype(bf16)
    table[2 * HB : 3 * HB] = (-signs).astype(bf16)
    lane_f = lane.astype(f32)

    def picked(ids_row):
        column = jnp.transpose(jnp.broadcast_to(ids_row.astype(f32), (HB, HB)))
        return jnp.where(column == lane_f, 1.0, 0.0).astype(bf16)

    def slot(y_, zl_):
        return pl.ds(pl.multiple_of(y_ * (2 * PR) + zl_ * PR, PR), PR)

    def group(c_, y_):
        return pl.ds(pl.multiple_of(c_ * PLANE + y_ * (2 * PR), 2 * PR), 2 * PR)

    def piece(p):
        return pl.ds(pl.multiple_of(p * PR, PR), PR)

    sends = (
        (None, z_peer),
        (None, y_next),
        (None, y_prev),
        (slot(y, 1 - zl), y_next),
        (slot(y, 1 - zl), y_prev),
        (slot(yp, 1), y_next),
        (slot(yn, 0), y_prev),
        (group(c, y), sibling),
        (group(c, yp), sibling),
        (group(c, yn), sibling),
        (group(c, y2), sibling),
    )
    comes = (
        slot(y, 1 - zl),
        slot(yp, zl),
        slot(yn, zl),
        slot(yp, 1 - zl),
        slot(yn, 1 - zl),
        slot(y2, 1),
        slot(y2, 0),
        group(1 - c, y),
        group(1 - c, yp),
        group(1 - c, yn),
        group(1 - c, y2),
    )

    def ag(kind, p):
        rows, peer = sends[kind]
        buffer = xr if kind < 7 else xg
        if kind < 3:
            rows = slot(y, zl)
            source = x_hbm.at[piece(p)]
        else:
            source = buffer.at[p, rows]
        return pltpu.make_async_remote_copy(
            src_ref=source, dst_ref=buffer.at[p, rows],
            send_sem=ag_s.at[p, kind], recv_sem=ag_r.at[p, kind],
            device_id=peer, device_id_type=MESH,
        )

    def ag_wait(kind, p):
        rows, peer = comes[kind], sends[kind][1]
        buffer = xr if kind < 7 else xg
        pltpu.make_async_remote_copy(
            src_ref=buffer.at[p, rows], dst_ref=buffer.at[p, rows],
            send_sem=ag_s.at[p, kind], recv_sem=ag_r.at[p, kind],
            device_id=peer, device_id_type=MESH,
        ).wait_recv()

    def st_copy(j):
        return pltpu.make_async_remote_copy(
            src_ref=st_out, dst_ref=st_in.at[j], send_sem=st_s.at[j], recv_sem=st_r.at[j],
            device_id=dev(dd=j + 1), device_id_type=MESH,
        )

    def tok_copy(j):
        return pltpu.make_async_remote_copy(
            src_ref=tok_out, dst_ref=tok_in.at[j], send_sem=tok_s.at[j], recv_sem=tok_r.at[j],
            device_id=plane_peers[j], device_id_type=MESH,
        )

    def stat(i, carry):
        rows = pl.ds(pl.multiple_of(i * 16, 16), 16)
        v = xin[rows, :].astype(f32)
        sums = jnp.sum(v, axis=1, keepdims=True)
        squares = jnp.sum(v * v, axis=1, keepdims=True)
        stat_t[0, rows, :] = jnp.where(lane[0:16] == 0, sums, squares)
        return carry

    def stats_send():
        lax.fori_loop(0, TR // 16, stat, 0)
        st_out[...] = jnp.transpose(stat_t[0])[0:8, :]
        for j in range(3):
            st_copy(j).start()

    def stats_total():
        for j in range(3):
            st_copy(j).wait_recv()
        total = st_out[...] + st_in[0] + st_in[1] + st_in[2]
        mean = total[0:1, :] * (1.0 / D)
        var = total[1:2, :] * (1.0 / D) - mean * mean
        rstd = lax.rsqrt(var + epsilon)
        sub = lax.broadcasted_iota(jnp.int32, (8, HB), 0)
        tok_out[...] = jnp.where(sub == 0, mean, rstd)
        for j in range(7):
            tok_copy(j).start()

    def stats_spread(y_, zl_, value):
        rows = jnp.where(row < HB // 2, value[0:1, :], value[1:2, :])
        stat_t[y_ * 2 + zl_] = jnp.transpose(rows)

    def stats_come():
        stats_spread(y, zl, tok_out[...])
        for j, (a, b) in enumerate(plane):
            tok_copy(j).wait_recv()
            stats_spread((y + 4 - a) % 4, (zl + b) % 2, tok_in[j])

    def normalize(y_, zl_, p, values):
        i = y_ * 2 + zl_
        mean, rstd = stat_t[i, piece(p), 0:1], stat_t[i, piece(p), HB // 2 : HB // 2 + 1]
        v = (values.astype(f32) - mean) * rstd * gain[...] + shift[...]
        rows = pl.ds(pl.multiple_of(c * PLANE + y_ * (2 * PR) + zl_ * PR, PR), PR)
        xg[p, rows, :] = v.astype(bf16)

    def half(h, dest):
        return pl.ds(pl.multiple_of(h * PLANE + dest * (2 * PR), 2 * PR), 2 * PR)

    dn, dq, d2 = (d + 1) % 4, (d + 3) % 4, (d + 2) % 4

    def part(f):
        return pl.ds(*PARTS[f])

    def first(way, f, p):
        return pltpu.make_async_remote_copy(
            src_ref=pbuf.at[p, half(1 - way, d2), part(f)], dst_ref=m1.at[p, way, :, part(f)],
            send_sem=m1_s.at[p, way, f], recv_sem=m1_r.at[p, way, f],
            device_id=dev(dd=1 if way == 0 else 3), device_id_type=MESH,
        )

    def second(way, h, f, p):
        return pltpu.make_async_remote_copy(
            src_ref=pbuf.at[p, half(h, dn if way == 0 else dq), part(f)], dst_ref=m2.at[p, way, h, :, part(f)],
            send_sem=m2_s.at[p, way, h, f], recv_sem=m2_r.at[p, way, h, f],
            device_id=dev(dd=1 if way == 0 else 3), device_id_type=MESH,
        )

    def wire(f, p):
        return pltpu.make_async_remote_copy(
            src_ref=wout.at[p, :, part(f)], dst_ref=win.at[p, :, part(f)], send_sem=wr_s.at[p, f], recv_sem=wr_r.at[p, f],
            device_id=dev(ds=1), device_id_type=MESH,
        )

    def grad_wire(g):
        return pltpu.make_async_remote_copy(
            src_ref=gwout.at[g], dst_ref=gwin.at[g], send_sem=gw_s.at[g], recv_sem=gw_r.at[g],
            device_id=dev(ds=3), device_id_type=MESH,
        )

    def own_rows(p):
        rows = pl.ds(pl.multiple_of(p * PR, PR), PR)
        return jnp.concatenate([oha[0, rows], oha[2, rows], oha[1, rows], oha[3, rows]], axis=0)

    def stage_own(p):
        ag(0, p).start()

    def stage_next(p):
        ag(1, p).start()
        ag(2, p).start()

    def stage_near(p):
        ag_wait(0, p)
        ag(3, p).start()
        ag(4, p).start()
        ag_wait(1, p)
        ag_wait(2, p)

        @pl.when(zl == 1)
        def _():
            ag(5, p).start()

        @pl.when(zl == 0)
        def _():
            ag(6, p).start()

    def stage_far(p):
        ag_wait(3, p)
        ag_wait(4, p)

        @pl.when(zl == 0)
        def _():
            ag(5, p).start()

        @pl.when(zl == 1)
        def _():
            ag(6, p).start()

    def stage_normalize(p):
        normalize(y, zl, p, xin[piece(p), :])
        normalize(y, 1 - zl, p, xr[p, slot(y, 1 - zl), :])
        ag(7, p).start()
        for kind, y_ in ((8, yp), (9, yn)):
            for zl_ in (0, 1):
                normalize(y_, zl_, p, xr[p, slot(y_, zl_), :])
            ag(kind, p).start()

    def stage_opposite(p):
        ag_wait(5, p)
        ag_wait(6, p)
        for zl_ in (0, 1):
            normalize(y2, zl_, p, xr[p, slot(y2, zl_), :])
        ag(10, p).start()

    def stage_product(p):
        for kind in (7, 8, 9, 10):
            ag_wait(kind, p)
        for f in range(2):
            pbuf[p, :, part(f)] = dot(xg[p], w[:, part(f)]).astype(bf16)
            first(0, f, p).start()
            first(1, f, p).start()
            second(0, 0, f, p).start()
            second(1, 1, f, p).start()

    def stage_sum(p):
        for f in range(2):
            for way in (0, 1):
                first(way, f, p).wait_recv()
                rows = half(1 - way, dn if way == 0 else dq)
                pbuf[p, rows, part(f)] = (
                    pbuf[p, rows, part(f)].astype(f32) + m1[p, way, :, part(f)].astype(f32)
                ).astype(bf16)
                second(way, 1 - way, f, p).start()

    def stage_code(p):
        for f in range(2):
            for way in (0, 1):
                for h in (0, 1):
                    second(way, h, f, p).wait_recv()
            parts = []
            for h in (0, 1):
                parts.append(
                    pbuf[p, half(h, d), part(f)].astype(f32)
                    + m2[p, 0, h, :, part(f)].astype(f32)
                    + m2[p, 1, h, :, part(f)].astype(f32)
                )
            delta = jnp.concatenate(parts, axis=0) + bias[:, part(f)] - dot(own_rows(p), sent[:, part(f)])
            for b in range(PARTS[f][1] // HB):
                columns = slice(b * HB, (b + 1) * HB)
                high = delta[:, columns].astype(bf16)
                low = (delta[:, columns] - high.astype(f32)).astype(bf16)
                tu = dot(jnp.concatenate([high, low], axis=1), table[0 : 2 * HB])
                wout[p, :, pl.ds(PARTS[f][0] + b * HB, HB)] = clipped(tu)
            wire(f, p).start()

    def stage_decode(p):
        chosen = own_rows(p)
        rows = pl.ds(pl.multiple_of(p * PR, PR), PR)
        for f in range(2):
            wire(f, p).wait_recv()
            for b in range(PARTS[f][1] // HB):
                columns = pl.ds(PARTS[f][0] + b * HB, HB)
                value = dot(
                    jnp.concatenate([chosen, win[p, :, columns]], axis=1),
                    jnp.concatenate([held[:, columns], table[0:HB]], axis=0),
                ).astype(bf16)
                for i, q in enumerate((0, 2, 1, 3)):
                    obuf[q, rows, columns] = value[i * PR : (i + 1) * PR]

    def stage_grad(g):
        for b in range(GB):
            columns = pl.ds(pl.multiple_of(g * GC + b * HB, HB), HB)
            stored = dot(ohg[...], bs[:, columns]).astype(bf16)
            tu = dot(jnp.concatenate([gi[:, columns], stored], axis=1), table[HB : 3 * HB])
            gwout[g, :, b * HB : (b + 1) * HB] = clipped(tu)
        grad_wire(g).start()

    def stage_grad_decode(g):
        grad_wire(g).wait_recv()
        for b in range(GB):
            columns = pl.ds(pl.multiple_of(g * GC + b * HB, HB), HB)
            gobuf[:, columns] = dot(
                jnp.concatenate([ohg[...], gwin[g, :, b * HB : (b + 1) * HB]], axis=1),
                jnp.concatenate([bh[:, columns], table[0:HB]], axis=0),
            ).astype(bf16)

    def stage_finish(p):
        for kind in range(11):
            ag(kind, p).wait_send()
        for f in range(2):
            for way in (0, 1):
                first(way, f, p).wait_send()
                for h in (0, 1):
                    second(way, h, f, p).wait_send()
            wire(f, p).wait_send()

    def stage_finish_grad(g):
        grad_wire(g).wait_send()

    def at(k, delay, stage, count=PIECES):
        p = k - delay

        @pl.when((p >= 0) & (p < count))
        def _():
            stage(p)

    def tick(k, carry):
        at(k, 2, stage_opposite)
        at(k, 1, stage_far)
        at(k, 0, stage_near)
        at(k, -AHEAD, stage_next)

        @pl.when(k == 0)
        def _():
            stats_total()
            lax.fori_loop(AHEAD, PIECES, own, 0)

        @pl.when(k == 1)
        def _():
            stats_come()

        at(k, 1, stage_normalize)

        @pl.when(k == 2)
        def _():
            for load in loads[8:]:
                load.wait()

        at(k, 2, stage_product)
        at(k, 3, stage_sum)
        at(k, CODE_DELAY, stage_code)
        at(k, CODE_DELAY + 1, stage_decode)
        at(k, GRAD_DELAY, stage_grad, GSTEPS)
        at(k, GRAD_DELAY + 3, stage_grad_decode, GSTEPS)
        at(k, GRAD_DELAY + 4, stage_finish_grad, GSTEPS)
        at(k, CODE_DELAY + 1, stage_finish, PIECES - 1)
        return carry

    def own(p, carry):
        stage_own(p)
        return carry

    pl.semaphore_wait(barrier, len(peers))
    for p in range(AHEAD):
        stage_own(p)
        stage_next(p)
    loads[0].wait()
    stats_send()
    for load in loads[6:]:
        load.start()
    for load in loads[1:6]:
        load.wait()
    for q in range(4):
        oha[q] = picked(aids[q : q + 1, :])
    ohg[...] = picked(gids[0:1, :])
    loads[6].wait()
    loads[7].wait()
    lax.fori_loop(0, PIECES + CODE_DELAY + 1, tick, 0)
    for j in range(7):
        tok_copy(j).wait_send()
    for j in range(3):
        st_copy(j).wait_send()

    stage_finish(PIECES - 1)


def shards(
    act_input, ln_gain, ln_shift, w_proj, b_proj, act_ids, sent_copy, held_copy,
    grad_input, grad_ids, back_sent, back_held,
):
    anywhere = pl.BlockSpec(memory_space=pl.ANY)
    vmem = pl.BlockSpec(memory_space=pltpu.VMEM)
    dma = pltpu.SemaphoreType.DMA
    arrived, grad_arrived = pl.pallas_call(
        kernel,
        out_shape=(
            pltpu.VMEM((4, TR, ND), bf16),
            pltpu.VMEM((TR, KD), bf16),
        ),
        in_specs=[anywhere] * 12,
        out_specs=(vmem, vmem),
        scratch_shapes=[
            pltpu.VMEM((TR, KD), bf16),
            pltpu.VMEM((1, KD), f32),
            pltpu.VMEM((1, KD), f32),
            pltpu.VMEM((1, ND), f32),
            pltpu.VMEM((4, TR), jnp.int32),
            pltpu.VMEM((1, TR), jnp.int32),
            pltpu.VMEM((KD, ND), bf16),
            pltpu.VMEM((HB, ND), bf16),
            pltpu.VMEM((HB, ND), bf16),
            pltpu.VMEM((TR, KD), bf16),
            pltpu.VMEM((HB, KD), bf16),
            pltpu.VMEM((HB, KD), bf16),
            pltpu.VMEM((PIECES, PLANE, KD), bf16),
            pltpu.VMEM((PIECES, 2 * PLANE, KD), bf16),
            pltpu.VMEM((PIECES, 2 * PLANE, ND), bf16),
            pltpu.VMEM((PIECES, 2, 2 * PR, ND), bf16),
            pltpu.VMEM((PIECES, 2, 2, 2 * PR, ND), bf16),
            pltpu.VMEM((PIECES, 4 * PR, ND), bf16),
            pltpu.VMEM((PIECES, 4 * PR, ND), bf16),
            pltpu.VMEM((GSTEPS, TR, GC), bf16),
            pltpu.VMEM((GSTEPS, TR, GC), bf16),
            pltpu.VMEM((3 * HB, HB), bf16),
            pltpu.VMEM((4, TR, HB), bf16),
            pltpu.VMEM((TR, HB), bf16),
            pltpu.VMEM((8, HB), f32),
            pltpu.VMEM((3, 8, HB), f32),
            pltpu.VMEM((8, HB), f32),
            pltpu.VMEM((7, 8, HB), f32),
            pltpu.VMEM((8, TR, HB), f32),
            dma((12,)),
            dma((PIECES, 11)),
            dma((PIECES, 11)),
            dma((PIECES, 2, 2)),
            dma((PIECES, 2, 2)),
            dma((PIECES, 2, 2, 2)),
            dma((PIECES, 2, 2, 2)),
            dma((PIECES, 2)),
            dma((PIECES, 2)),
            dma((GSTEPS,)),
            dma((GSTEPS,)),
            dma((3,)),
            dma((3,)),
            dma((7,)),
            dma((7,)),
        ],
        compiler_params=pltpu.CompilerParams(
            collective_id=0, has_side_effects=True, vmem_limit_bytes=56 * 2**20
        ),
        cost_estimate=pl.CostEstimate(
            flops=2 * 2048 * KD * ND, bytes_accessed=14 * 2**20, transcendentals=0
        ),
        name="relay",
    )(
        act_input[0], ln_gain, ln_shift, w_proj[0], b_proj, act_ids.reshape(4, TR),
        sent_copy[0], held_copy[0], grad_input[0], grad_ids.reshape(1, TR), back_sent[0], back_held[0],
    )
    return (arrived.reshape(1, 4 * TR, ND), grad_arrived[None])


def solution(mesh):
    placed = (
        P("section", "tensor", "dp"),
        P("section", "dp"),
        P("section", "dp"),
        P("section", "dp", "tensor"),
        P("section", "tensor"),
        P("dp"),
        P("section", "dp", "tensor"),
        P("section", "dp", "tensor"),
        P("section", "tensor", "dp"),
        P("tensor"),
        P("section", "tensor", "dp"),
        P("section", "tensor", "dp"),
    )
    return jax.shard_map(
        shards,
        mesh=mesh,
        in_specs=placed,
        out_specs=(P("section", "dp", "tensor"), P("section", "tensor", "dp")),
        check_vma=False,
    )
```

```python
import functools
import math

import jax
import jax.numpy as jnp
from jax import lax
from jax.experimental import pallas as pl
from jax.experimental.pallas import tpu as pltpu
from jax.sharding import PartitionSpec as P

D = 14336
HB = 128
KD = 3584
ND = 896
TR = 128
PIECES = 8
PR = TR // PIECES
PLANE = 8 * PR
GB = 4
GSTEPS = KD // (HB * GB)
GC = GB * HB
AHEAD = 2
CODE_DELAY = 5
GRAD_DELAY = 1
PARTS = ((0, 512), (512, 384))

epsilon = 1e-05
scale_epsilon = 1e-06
clip_level = 2.5

MESH = pl.DeviceIdType.MESH
f32 = jnp.float32
bf16 = jnp.bfloat16


def dot(a, b):
    return jnp.dot(a, b, preferred_element_type=f32)


def clipped(tu):
    mean = jnp.sum(tu * tu, axis=1, keepdims=True) * (1.0 / (HB * HB))
    scale = jnp.sqrt(mean + scale_epsilon).astype(bf16).astype(f32)
    bound = scale * (clip_level / math.sqrt(HB))
    return jnp.clip(tu * (1.0 / HB), -bound, bound).astype(bf16)


def kernel(
    x_hbm, gain_hbm, shift_hbm, w_hbm, bias_hbm, aids_hbm, sent_hbm, held_hbm, gi_hbm, gids_hbm, bs_hbm, bh_hbm,
    obuf, gobuf,
    xin, gain, shift, bias, aids, gids, w, sent, held, gi, bs, bh, xr, xg, pbuf, m1, m2, wout, win, gwout, gwin,
    table, oha, ohg, st_out, st_in, tok_out, tok_in, stat_t,
    lsem, ag_s, ag_r, m1_s, m1_r, m2_s, m2_r, wr_s, wr_r, gw_s, gw_r, st_s, st_r, tok_s, tok_r,
):
    s = lax.axis_index("section")
    d = lax.axis_index("dp")
    t = lax.axis_index("tensor")
    y = t // 4
    zl = (t // 2) % 2
    c = t % 2
    yn, yp = (y + 1) % 4, (y + 3) % 4
    y2 = (y + 2) % 4

    def dev(ds=0, dd=0, y_=None, zl_=None, c_=None):
        y_ = y if y_ is None else y_
        zl_ = zl if zl_ is None else zl_
        c_ = c if c_ is None else c_
        return ((s + ds) % 4, (d + dd) % 4, y_ * 4 + zl_ * 2 + c_)

    z_peer = dev(zl_=1 - zl)
    y_next, y_prev = dev(y_=yn), dev(y_=yp)
    sibling = dev(c_=1 - c)

    loads = [
        pltpu.make_async_copy(a, b, lsem.at[i])
        for i, (a, b) in enumerate(
            (
                (x_hbm, xin), (aids_hbm, aids), (gids_hbm, gids), (gain_hbm, gain), (shift_hbm, shift), (bias_hbm, bias),
                (gi_hbm, gi), (bs_hbm, bs), (w_hbm, w), (sent_hbm, sent), (held_hbm, held), (bh_hbm, bh),
            )
        )
    ]
    barrier = pltpu.get_barrier_semaphore()
    plane = [(0, 1), (1, 0), (3, 0), (1, 1), (3, 1), (2, 0), (2, 1)]
    plane_peers = [dev(y_=(y + a) % 4, zl_=(zl + b) % 2) for a, b in plane]
    peers = plane_peers + [sibling, dev(dd=1), dev(dd=2), dev(dd=3), dev(ds=1), dev(ds=3)]
    peers += [dev(ds=a, dd=b) for a in (1, 3) for b in (1, 3)]
    for peer in peers:
        pl.semaphore_signal(barrier, inc=1, device_id=peer, device_id_type=MESH)
    for load in loads[0:6]:
        load.start()

    row = lax.broadcasted_iota(jnp.int32, (HB, HB), 0)
    lane = lax.broadcasted_iota(jnp.int32, (HB, HB), 1)
    both = row & lane
    both = both ^ (both >> 4)
    both = both ^ (both >> 2)
    both = both ^ (both >> 1)
    signs = (1 - 2 * (both & 1)).astype(f32)
    table[0:HB] = signs.astype(bf16)
    table[HB : 2 * HB] = signs.astype(bf16)
    table[2 * HB : 3 * HB] = (-signs).astype(bf16)
    lane_f = lane.astype(f32)

    def picked(ids_row):
        column = jnp.transpose(jnp.broadcast_to(ids_row.astype(f32), (HB, HB)))
        return jnp.where(column == lane_f, 1.0, 0.0).astype(bf16)

    def slot(y_, zl_):
        return pl.ds(pl.multiple_of(y_ * (2 * PR) + zl_ * PR, PR), PR)

    def group(c_, y_):
        return pl.ds(pl.multiple_of(c_ * PLANE + y_ * (2 * PR), 2 * PR), 2 * PR)

    def piece(p):
        return pl.ds(pl.multiple_of(p * PR, PR), PR)

    sends = (
        (None, z_peer),
        (None, y_next),
        (None, y_prev),
        (slot(y, 1 - zl), y_next),
        (slot(y, 1 - zl), y_prev),
        (slot(yp, 1), y_next),
        (slot(yn, 0), y_prev),
        (group(c, y), sibling),
        (group(c, yp), sibling),
        (group(c, yn), sibling),
        (group(c, y2), sibling),
    )
    comes = (
        slot(y, 1 - zl),
        slot(yp, zl),
        slot(yn, zl),
        slot(yp, 1 - zl),
        slot(yn, 1 - zl),
        slot(y2, 1),
        slot(y2, 0),
        group(1 - c, y),
        group(1 - c, yp),
        group(1 - c, yn),
        group(1 - c, y2),
    )

    def ag(kind, p):
        rows, peer = sends[kind]
        buffer = xr if kind < 7 else xg
        if kind < 3:
            rows = slot(y, zl)
            source = x_hbm.at[piece(p)]
        else:
            source = buffer.at[p, rows]
        return pltpu.make_async_remote_copy(
            src_ref=source, dst_ref=buffer.at[p, rows],
            send_sem=ag_s.at[p, kind], recv_sem=ag_r.at[p, kind],
            device_id=peer, device_id_type=MESH,
        )

    def ag_wait(kind, p):
        rows, peer = comes[kind], sends[kind][1]
        buffer = xr if kind < 7 else xg
        pltpu.make_async_remote_copy(
            src_ref=buffer.at[p, rows], dst_ref=buffer.at[p, rows],
            send_sem=ag_s.at[p, kind], recv_sem=ag_r.at[p, kind],
            device_id=peer, device_id_type=MESH,
        ).wait_recv()

    def st_copy(j):
        return pltpu.make_async_remote_copy(
            src_ref=st_out, dst_ref=st_in.at[j], send_sem=st_s.at[j], recv_sem=st_r.at[j],
            device_id=dev(dd=j + 1), device_id_type=MESH,
        )

    def tok_copy(j):
        return pltpu.make_async_remote_copy(
            src_ref=tok_out, dst_ref=tok_in.at[j], send_sem=tok_s.at[j], recv_sem=tok_r.at[j],
            device_id=plane_peers[j], device_id_type=MESH,
        )

    def stat(i, carry):
        rows = pl.ds(pl.multiple_of(i * 16, 16), 16)
        v = xin[rows, :].astype(f32)
        sums = jnp.sum(v, axis=1, keepdims=True)
        squares = jnp.sum(v * v, axis=1, keepdims=True)
        stat_t[0, rows, :] = jnp.where(lane[0:16] == 0, sums, squares)
        return carry

    def stats_send():
        lax.fori_loop(0, TR // 16, stat, 0)
        st_out[...] = jnp.transpose(stat_t[0])[0:8, :]
        for j in range(3):
            st_copy(j).start()

    def stats_total():
        for j in range(3):
            st_copy(j).wait_recv()
        total = st_out[...] + st_in[0] + st_in[1] + st_in[2]
        mean = total[0:1, :] * (1.0 / D)
        var = total[1:2, :] * (1.0 / D) - mean * mean
        rstd = lax.rsqrt(var + epsilon)
        sub = lax.broadcasted_iota(jnp.int32, (8, HB), 0)
        tok_out[...] = jnp.where(sub == 0, mean, rstd)
        for j in range(7):
            tok_copy(j).start()

    def stats_spread(y_, zl_, value):
        rows = jnp.where(row < HB // 2, value[0:1, :], value[1:2, :])
        stat_t[y_ * 2 + zl_] = jnp.transpose(rows)

    def stats_come():
        stats_spread(y, zl, tok_out[...])
        for j, (a, b) in enumerate(plane):
            tok_copy(j).wait_recv()
            stats_spread((y + 4 - a) % 4, (zl + b) % 2, tok_in[j])

    def normalize(y_, zl_, p, values):
        i = y_ * 2 + zl_
        mean, rstd = stat_t[i, piece(p), 0:1], stat_t[i, piece(p), HB // 2 : HB // 2 + 1]
        v = (values.astype(f32) - mean) * rstd * gain[...] + shift[...]
        rows = pl.ds(pl.multiple_of(c * PLANE + y_ * (2 * PR) + zl_ * PR, PR), PR)
        xg[p, rows, :] = v.astype(bf16)

    def half(h, dest):
        return pl.ds(pl.multiple_of(h * PLANE + dest * (2 * PR), 2 * PR), 2 * PR)

    dn, dq, d2 = (d + 1) % 4, (d + 3) % 4, (d + 2) % 4

    def part(f):
        return pl.ds(*PARTS[f])

    def first(way, f, p):
        return pltpu.make_async_remote_copy(
            src_ref=pbuf.at[p, half(1 - way, d2), part(f)], dst_ref=m1.at[p, way, :, part(f)],
            send_sem=m1_s.at[p, way, f], recv_sem=m1_r.at[p, way, f],
            device_id=dev(dd=1 if way == 0 else 3), device_id_type=MESH,
        )

    def second(way, h, f, p):
        return pltpu.make_async_remote_copy(
            src_ref=pbuf.at[p, half(h, dn if way == 0 else dq), part(f)], dst_ref=m2.at[p, way, h, :, part(f)],
            send_sem=m2_s.at[p, way, h, f], recv_sem=m2_r.at[p, way, h, f],
            device_id=dev(ds=1, dd=1 if way == 0 else 3), device_id_type=MESH,
        )

    def base(f, p):
        return pltpu.make_async_remote_copy(
            src_ref=wout.at[p, :, part(f)], dst_ref=win.at[p, :, part(f)], send_sem=wr_s.at[p, f], recv_sem=wr_r.at[p, f],
            device_id=dev(ds=1), device_id_type=MESH,
        )

    def grad_wire(g):
        return pltpu.make_async_remote_copy(
            src_ref=gwout.at[g], dst_ref=gwin.at[g], send_sem=gw_s.at[g], recv_sem=gw_r.at[g],
            device_id=dev(ds=3), device_id_type=MESH,
        )

    def own_rows(p):
        rows = pl.ds(pl.multiple_of(p * PR, PR), PR)
        return jnp.concatenate([oha[0, rows], oha[2, rows], oha[1, rows], oha[3, rows]], axis=0)

    def stage_own(p):
        ag(0, p).start()

    def stage_next(p):
        ag(1, p).start()
        ag(2, p).start()

    def stage_near(p):
        ag_wait(0, p)
        ag(3, p).start()
        ag(4, p).start()
        ag_wait(1, p)
        ag_wait(2, p)

        @pl.when(zl == 1)
        def _():
            ag(5, p).start()

        @pl.when(zl == 0)
        def _():
            ag(6, p).start()

    def stage_far(p):
        ag_wait(3, p)
        ag_wait(4, p)

        @pl.when(zl == 0)
        def _():
            ag(5, p).start()

        @pl.when(zl == 1)
        def _():
            ag(6, p).start()

    def stage_normalize(p):
        normalize(y, zl, p, xin[piece(p), :])
        normalize(y, 1 - zl, p, xr[p, slot(y, 1 - zl), :])
        ag(7, p).start()
        for kind, y_ in ((8, yp), (9, yn)):
            for zl_ in (0, 1):
                normalize(y_, zl_, p, xr[p, slot(y_, zl_), :])
            ag(kind, p).start()

    def stage_opposite(p):
        ag_wait(5, p)
        ag_wait(6, p)
        for zl_ in (0, 1):
            normalize(y2, zl_, p, xr[p, slot(y2, zl_), :])
        ag(10, p).start()

    def stage_product(p):
        for kind in (7, 8, 9, 10):
            ag_wait(kind, p)
        chosen = own_rows(p)
        for f in range(2):
            pbuf[p, :, part(f)] = dot(xg[p], w[:, part(f)]).astype(bf16)
            first(0, f, p).start()
            first(1, f, p).start()
            second(0, 0, f, p).start()
            second(1, 1, f, p).start()
            own = jnp.concatenate([pbuf[p, half(0, d), part(f)], pbuf[p, half(1, d), part(f)]], axis=0)
            wout[p, :, part(f)] = (own.astype(f32) + (bias[:, part(f)] - dot(chosen, sent[:, part(f)]))).astype(bf16)
            base(f, p).start()

    def stage_sum(p):
        for f in range(2):
            for way in (0, 1):
                first(way, f, p).wait_recv()
                rows = half(1 - way, dn if way == 0 else dq)
                pbuf[p, rows, part(f)] = (
                    pbuf[p, rows, part(f)].astype(f32) + m1[p, way, :, part(f)].astype(f32)
                ).astype(bf16)
                second(way, 1 - way, f, p).start()

    def stage_code(p):
        chosen = own_rows(p)
        rows = pl.ds(pl.multiple_of(p * PR, PR), PR)
        for f in range(2):
            base(f, p).wait_recv()
            for way in (0, 1):
                for h in (0, 1):
                    second(way, h, f, p).wait_recv()
            for b in range(PARTS[f][1] // HB):
                columns = pl.ds(PARTS[f][0] + b * HB, HB)
                other = [m2[p, 0, h, :, columns].astype(f32) + m2[p, 1, h, :, columns].astype(f32) for h in (0, 1)]
                delta = win[p, :, columns].astype(f32) + jnp.concatenate(other, axis=0)
                high = delta.astype(bf16)
                low = (delta - high.astype(f32)).astype(bf16)
                coded = clipped(dot(jnp.concatenate([high, low], axis=1), table[0 : 2 * HB]))
                value = dot(
                    jnp.concatenate([chosen, coded], axis=1),
                    jnp.concatenate([held[:, columns], table[0:HB]], axis=0),
                ).astype(bf16)
                for i, q in enumerate((0, 2, 1, 3)):
                    obuf[q, rows, columns] = value[i * PR : (i + 1) * PR]

    def stage_grad(g):
        for b in range(GB):
            columns = pl.ds(pl.multiple_of(g * GC + b * HB, HB), HB)
            stored = dot(ohg[...], bs[:, columns]).astype(bf16)
            tu = dot(jnp.concatenate([gi[:, columns], stored], axis=1), table[HB : 3 * HB])
            gwout[g, :, b * HB : (b + 1) * HB] = clipped(tu)
        grad_wire(g).start()

    def stage_grad_decode(g):
        grad_wire(g).wait_recv()
        for b in range(GB):
            columns = pl.ds(pl.multiple_of(g * GC + b * HB, HB), HB)
            gobuf[:, columns] = dot(
                jnp.concatenate([ohg[...], gwin[g, :, b * HB : (b + 1) * HB]], axis=1),
                jnp.concatenate([bh[:, columns], table[0:HB]], axis=0),
            ).astype(bf16)

    def stage_finish(p):
        for kind in range(11):
            ag(kind, p).wait_send()
        for f in range(2):
            for way in (0, 1):
                first(way, f, p).wait_send()
                for h in (0, 1):
                    second(way, h, f, p).wait_send()
            base(f, p).wait_send()

    def stage_finish_grad(g):
        grad_wire(g).wait_send()

    def at(k, delay, stage, count=PIECES):
        p = k - delay

        @pl.when((p >= 0) & (p < count))
        def _():
            stage(p)

    def tick(k, carry):
        at(k, 2, stage_opposite)
        at(k, 1, stage_far)
        at(k, 0, stage_near)
        at(k, -AHEAD, stage_next)

        @pl.when(k == 0)
        def _():
            stats_total()
            lax.fori_loop(AHEAD, PIECES, own, 0)

        @pl.when(k == 1)
        def _():
            stats_come()

        at(k, 1, stage_normalize)

        @pl.when(k == 2)
        def _():
            for load in loads[8:]:
                load.wait()

        at(k, 2, stage_product)
        at(k, 3, stage_sum)
        at(k, CODE_DELAY, stage_code)
        at(k, GRAD_DELAY, stage_grad, GSTEPS)
        at(k, GRAD_DELAY + 2, stage_grad_decode, GSTEPS)
        at(k, GRAD_DELAY + 3, stage_finish_grad, GSTEPS)
        at(k, CODE_DELAY, stage_finish, PIECES - 1)
        return carry

    def own(p, carry):
        stage_own(p)
        return carry

    pl.semaphore_wait(barrier, len(peers))
    for p in range(AHEAD):
        stage_own(p)
        stage_next(p)
    loads[0].wait()
    stats_send()
    for load in loads[6:]:
        load.start()
    for load in loads[1:6]:
        load.wait()
    for q in range(4):
        oha[q] = picked(aids[q : q + 1, :])
    ohg[...] = picked(gids[0:1, :])
    loads[6].wait()
    loads[7].wait()
    lax.fori_loop(0, PIECES + CODE_DELAY, tick, 0)
    for j in range(7):
        tok_copy(j).wait_send()
    for j in range(3):
        st_copy(j).wait_send()

    stage_finish(PIECES - 1)


def shards(
    act_input, ln_gain, ln_shift, w_proj, b_proj, act_ids, sent_copy, held_copy,
    grad_input, grad_ids, back_sent, back_held,
):
    anywhere = pl.BlockSpec(memory_space=pl.ANY)
    vmem = pl.BlockSpec(memory_space=pltpu.VMEM)
    dma = pltpu.SemaphoreType.DMA
    arrived, grad_arrived = pl.pallas_call(
        kernel,
        out_shape=(
            pltpu.VMEM((4, TR, ND), bf16),
            pltpu.VMEM((TR, KD), bf16),
        ),
        in_specs=[anywhere] * 12,
        out_specs=(vmem, vmem),
        scratch_shapes=[
            pltpu.VMEM((TR, KD), bf16),
            pltpu.VMEM((1, KD), f32),
            pltpu.VMEM((1, KD), f32),
            pltpu.VMEM((1, ND), f32),
            pltpu.VMEM((4, TR), jnp.int32),
            pltpu.VMEM((1, TR), jnp.int32),
            pltpu.VMEM((KD, ND), bf16),
            pltpu.VMEM((HB, ND), bf16),
            pltpu.VMEM((HB, ND), bf16),
            pltpu.VMEM((TR, KD), bf16),
            pltpu.VMEM((HB, KD), bf16),
            pltpu.VMEM((HB, KD), bf16),
            pltpu.VMEM((PIECES, PLANE, KD), bf16),
            pltpu.VMEM((PIECES, 2 * PLANE, KD), bf16),
            pltpu.VMEM((PIECES, 2 * PLANE, ND), bf16),
            pltpu.VMEM((PIECES, 2, 2 * PR, ND), bf16),
            pltpu.VMEM((PIECES, 2, 2, 2 * PR, ND), bf16),
            pltpu.VMEM((PIECES, 4 * PR, ND), bf16),
            pltpu.VMEM((PIECES, 4 * PR, ND), bf16),
            pltpu.VMEM((GSTEPS, TR, GC), bf16),
            pltpu.VMEM((GSTEPS, TR, GC), bf16),
            pltpu.VMEM((3 * HB, HB), bf16),
            pltpu.VMEM((4, TR, HB), bf16),
            pltpu.VMEM((TR, HB), bf16),
            pltpu.VMEM((8, HB), f32),
            pltpu.VMEM((3, 8, HB), f32),
            pltpu.VMEM((8, HB), f32),
            pltpu.VMEM((7, 8, HB), f32),
            pltpu.VMEM((8, TR, HB), f32),
            dma((12,)),
            dma((PIECES, 11)),
            dma((PIECES, 11)),
            dma((PIECES, 2, 2)),
            dma((PIECES, 2, 2)),
            dma((PIECES, 2, 2, 2)),
            dma((PIECES, 2, 2, 2)),
            dma((PIECES, 2)),
            dma((PIECES, 2)),
            dma((GSTEPS,)),
            dma((GSTEPS,)),
            dma((3,)),
            dma((3,)),
            dma((7,)),
            dma((7,)),
        ],
        compiler_params=pltpu.CompilerParams(
            collective_id=0, has_side_effects=True, vmem_limit_bytes=56 * 2**20
        ),
        cost_estimate=pl.CostEstimate(
            flops=2 * 2048 * KD * ND, bytes_accessed=14 * 2**20, transcendentals=0
        ),
        name="relay",
    )(
        act_input[0], ln_gain, ln_shift, w_proj[0], b_proj, act_ids.reshape(4, TR),
        sent_copy[0], held_copy[0], grad_input[0], grad_ids.reshape(1, TR), back_sent[0], back_held[0],
    )
    return (arrived.reshape(1, 4 * TR, ND), grad_arrived[None])


def solution(mesh):
    placed = (
        P("section", "tensor", "dp"),
        P("section", "dp"),
        P("section", "dp"),
        P("section", "dp", "tensor"),
        P("section", "tensor"),
        P("dp"),
        P("section", "dp", "tensor"),
        P("section", "dp", "tensor"),
        P("section", "tensor", "dp"),
        P("tensor"),
        P("section", "tensor", "dp"),
        P("section", "tensor", "dp"),
    )
    return jax.shard_map(
        shards,
        mesh=mesh,
        in_specs=placed,
        out_specs=(P("section", "dp", "tensor"), P("section", "tensor", "dp")),
        check_vma=False,
    )
```

```python
import functools
import math

import jax
import jax.numpy as jnp
from jax import lax
from jax.experimental import pallas as pl
from jax.experimental.pallas import tpu as pltpu
from jax.sharding import PartitionSpec as P

D = 14336
HB = 128
KD = 3584
ND = 896
TR = 128
PIECES = 8
PR = TR // PIECES
PLANE = 8 * PR
GB = 4
GSTEPS = KD // (HB * GB)
GC = GB * HB
AHEAD = 2
CODE_DELAY = 5
GRAD_DELAY = 1
PARTS = ((0, 512), (512, 384))

epsilon = 1e-05
scale_epsilon = 1e-06
clip_level = 2.5

MESH = pl.DeviceIdType.MESH
f32 = jnp.float32
bf16 = jnp.bfloat16


def dot(a, b):
    return jnp.dot(a, b, preferred_element_type=f32)


def clipped(tu):
    mean = jnp.sum(tu * tu, axis=1, keepdims=True) * (1.0 / (HB * HB))
    scale = jnp.sqrt(mean + scale_epsilon).astype(bf16).astype(f32)
    bound = scale * (clip_level / math.sqrt(HB))
    return jnp.clip(tu * (1.0 / HB), -bound, bound).astype(bf16)


def kernel(
    x_hbm, gain_hbm, shift_hbm, w_hbm, bias_hbm, aids_hbm, sent_hbm, held_hbm, gi_hbm, gids_hbm, bs_hbm, bh_hbm,
    obuf, gobuf,
    xin, gain, shift, bias, aids, gids, w, sent, held, gi, bs, bh, xr, xg, pbuf, m1, m2, wout, win, gwout, gwin,
    table, oha, ohg, st_out, st_in, tok_out, tok_in, stat_t,
    lsem, ag_s, ag_r, m1_s, m1_r, m2_s, m2_r, wr_s, wr_r, gw_s, gw_r, st_s, st_r, tok_s, tok_r,
):
    s = lax.axis_index("section")
    d = lax.axis_index("dp")
    t = lax.axis_index("tensor")
    y = t // 4
    zl = (t // 2) % 2
    c = t % 2
    yn, yp = (y + 1) % 4, (y + 3) % 4
    y2 = (y + 2) % 4

    def dev(ds=0, dd=0, y_=None, zl_=None, c_=None):
        y_ = y if y_ is None else y_
        zl_ = zl if zl_ is None else zl_
        c_ = c if c_ is None else c_
        return ((s + ds) % 4, (d + dd) % 4, y_ * 4 + zl_ * 2 + c_)

    z_peer = dev(zl_=1 - zl)
    y_next, y_prev = dev(y_=yn), dev(y_=yp)
    sibling = dev(c_=1 - c)

    loads = [
        pltpu.make_async_copy(a, b, lsem.at[i])
        for i, (a, b) in enumerate(
            (
                (x_hbm, xin), (aids_hbm, aids), (gids_hbm, gids), (gain_hbm, gain), (shift_hbm, shift), (bias_hbm, bias),
                (gi_hbm, gi), (bs_hbm, bs), (w_hbm, w), (sent_hbm, sent), (held_hbm, held), (bh_hbm, bh),
            )
        )
    ]
    barrier = pltpu.get_barrier_semaphore()
    plane = [(0, 1), (1, 0), (3, 0), (1, 1), (3, 1), (2, 0), (2, 1)]
    plane_peers = [dev(y_=(y + a) % 4, zl_=(zl + b) % 2) for a, b in plane]
    peers = plane_peers + [sibling, dev(dd=1), dev(dd=2), dev(dd=3), dev(ds=1), dev(ds=3)]
    peers += [dev(ds=a, dd=b) for a in (1, 3) for b in (1, 3)]
    for peer in peers:
        pl.semaphore_signal(barrier, inc=1, device_id=peer, device_id_type=MESH)
    for load in loads[0:6]:
        load.start()

    row = lax.broadcasted_iota(jnp.int32, (HB, HB), 0)
    lane = lax.broadcasted_iota(jnp.int32, (HB, HB), 1)
    both = row & lane
    both = both ^ (both >> 4)
    both = both ^ (both >> 2)
    both = both ^ (both >> 1)
    signs = (1 - 2 * (both & 1)).astype(f32)
    table[0:HB] = signs.astype(bf16)
    table[HB : 2 * HB] = signs.astype(bf16)
    table[2 * HB : 3 * HB] = (-signs).astype(bf16)
    lane_f = lane.astype(f32)

    def picked(ids_row):
        column = jnp.transpose(jnp.broadcast_to(ids_row.astype(f32), (HB, HB)))
        return jnp.where(column == lane_f, 1.0, 0.0).astype(bf16)

    def slot(y_, zl_):
        return pl.ds(pl.multiple_of(y_ * (2 * PR) + zl_ * PR, PR), PR)

    def group(c_, y_):
        return pl.ds(pl.multiple_of(c_ * PLANE + y_ * (2 * PR), 2 * PR), 2 * PR)

    def piece(p):
        return pl.ds(pl.multiple_of(p * PR, PR), PR)

    sends = (
        (None, z_peer),
        (None, y_next),
        (None, y_prev),
        (slot(y, 1 - zl), y_next),
        (slot(y, 1 - zl), y_prev),
        (slot(yp, 1), y_next),
        (slot(yn, 0), y_prev),
        (group(c, y), sibling),
        (group(c, yp), sibling),
        (group(c, yn), sibling),
        (group(c, y2), sibling),
    )
    comes = (
        slot(y, 1 - zl),
        slot(yp, zl),
        slot(yn, zl),
        slot(yp, 1 - zl),
        slot(yn, 1 - zl),
        slot(y2, 1),
        slot(y2, 0),
        group(1 - c, y),
        group(1 - c, yp),
        group(1 - c, yn),
        group(1 - c, y2),
    )

    def ag(kind, p):
        rows, peer = sends[kind]
        buffer = xr if kind < 7 else xg
        if kind < 3:
            rows = slot(y, zl)
            source = x_hbm.at[piece(p)]
        else:
            source = buffer.at[p, rows]
        return pltpu.make_async_remote_copy(
            src_ref=source, dst_ref=buffer.at[p, rows],
            send_sem=ag_s.at[p, kind], recv_sem=ag_r.at[p, kind],
            device_id=peer, device_id_type=MESH,
        )

    def ag_wait(kind, p):
        rows, peer = comes[kind], sends[kind][1]
        buffer = xr if kind < 7 else xg
        pltpu.make_async_remote_copy(
            src_ref=buffer.at[p, rows], dst_ref=buffer.at[p, rows],
            send_sem=ag_s.at[p, kind], recv_sem=ag_r.at[p, kind],
            device_id=peer, device_id_type=MESH,
        ).wait_recv()

    def st_copy(j):
        return pltpu.make_async_remote_copy(
            src_ref=st_out, dst_ref=st_in.at[j], send_sem=st_s.at[j], recv_sem=st_r.at[j],
            device_id=dev(dd=j + 1), device_id_type=MESH,
        )

    def tok_copy(j):
        return pltpu.make_async_remote_copy(
            src_ref=tok_out, dst_ref=tok_in.at[j], send_sem=tok_s.at[j], recv_sem=tok_r.at[j],
            device_id=plane_peers[j], device_id_type=MESH,
        )

    def stat(i, carry):
        rows = pl.ds(pl.multiple_of(i * 16, 16), 16)
        v = xin[rows, :].astype(f32)
        sums = jnp.sum(v, axis=1, keepdims=True)
        squares = jnp.sum(v * v, axis=1, keepdims=True)
        stat_t[0, rows, :] = jnp.where(lane[0:16] == 0, sums, squares)
        return carry

    def stats_send():
        lax.fori_loop(0, TR // 16, stat, 0)
        st_out[...] = jnp.transpose(stat_t[0])[0:8, :]
        for j in range(3):
            st_copy(j).start()

    def stats_total():
        for j in range(3):
            st_copy(j).wait_recv()
        total = st_out[...] + st_in[0] + st_in[1] + st_in[2]
        mean = total[0:1, :] * (1.0 / D)
        var = total[1:2, :] * (1.0 / D) - mean * mean
        rstd = lax.rsqrt(var + epsilon)
        sub = lax.broadcasted_iota(jnp.int32, (8, HB), 0)
        tok_out[...] = jnp.where(sub == 0, mean, rstd)
        for j in range(7):
            tok_copy(j).start()

    def stats_spread(y_, zl_, value):
        rows = jnp.where(row < HB // 2, value[0:1, :], value[1:2, :])
        stat_t[y_ * 2 + zl_] = jnp.transpose(rows)

    def stats_come():
        stats_spread(y, zl, tok_out[...])
        for j, (a, b) in enumerate(plane):
            tok_copy(j).wait_recv()
            stats_spread((y + 4 - a) % 4, (zl + b) % 2, tok_in[j])

    def normalize(y_, zl_, p, values):
        i = y_ * 2 + zl_
        mean, rstd = stat_t[i, piece(p), 0:1], stat_t[i, piece(p), HB // 2 : HB // 2 + 1]
        v = (values.astype(f32) - mean) * rstd * gain[...] + shift[...]
        rows = pl.ds(pl.multiple_of(c * PLANE + y_ * (2 * PR) + zl_ * PR, PR), PR)
        xg[p, rows, :] = v.astype(bf16)

    def half(h, dest):
        return pl.ds(pl.multiple_of(h * PLANE + dest * (2 * PR), 2 * PR), 2 * PR)

    dn, dq, d2 = (d + 1) % 4, (d + 3) % 4, (d + 2) % 4

    def part(f):
        return pl.ds(*PARTS[f])

    def first(way, f, p):
        return pltpu.make_async_remote_copy(
            src_ref=pbuf.at[p, half(1 - way, d2), part(f)], dst_ref=m1.at[p, way, :, part(f)],
            send_sem=m1_s.at[p, way, f], recv_sem=m1_r.at[p, way, f],
            device_id=dev(dd=1 if way == 0 else 3), device_id_type=MESH,
        )

    def second(way, h, f, p):
        return pltpu.make_async_remote_copy(
            src_ref=pbuf.at[p, half(h, dn if way == 0 else dq), part(f)], dst_ref=m2.at[p, way, h, :, part(f)],
            send_sem=m2_s.at[p, way, h, f], recv_sem=m2_r.at[p, way, h, f],
            device_id=dev(ds=1, dd=1 if way == 0 else 3), device_id_type=MESH,
        )

    def base(f, p):
        return pltpu.make_async_remote_copy(
            src_ref=wout.at[p, :, part(f)], dst_ref=win.at[p, :, part(f)], send_sem=wr_s.at[p, f], recv_sem=wr_r.at[p, f],
            device_id=dev(ds=1), device_id_type=MESH,
        )

    def grad_wire(g):
        return pltpu.make_async_remote_copy(
            src_ref=gwout.at[g], dst_ref=gwin.at[g], send_sem=gw_s.at[g], recv_sem=gw_r.at[g],
            device_id=dev(ds=3), device_id_type=MESH,
        )

    def own_rows(p):
        rows = pl.ds(pl.multiple_of(p * PR, PR), PR)
        return jnp.concatenate([oha[0, rows], oha[2, rows], oha[1, rows], oha[3, rows]], axis=0)

    def stage_own(p):
        ag(0, p).start()

    def stage_next(p):
        ag(1, p).start()
        ag(2, p).start()

    def stage_near(p):
        ag_wait(0, p)
        ag(3, p).start()
        ag(4, p).start()
        ag_wait(1, p)
        ag_wait(2, p)

        @pl.when(zl == 1)
        def _():
            ag(5, p).start()

        @pl.when(zl == 0)
        def _():
            ag(6, p).start()

    def stage_far(p):
        ag_wait(3, p)
        ag_wait(4, p)

        @pl.when(zl == 0)
        def _():
            ag(5, p).start()

        @pl.when(zl == 1)
        def _():
            ag(6, p).start()

    def stage_normalize(p):
        normalize(y, zl, p, xin[piece(p), :])
        normalize(y, 1 - zl, p, xr[p, slot(y, 1 - zl), :])
        ag(7, p).start()
        for kind, y_ in ((8, yp), (9, yn)):
            for zl_ in (0, 1):
                normalize(y_, zl_, p, xr[p, slot(y_, zl_), :])
            ag(kind, p).start()

    def stage_opposite(p):
        ag_wait(5, p)
        ag_wait(6, p)
        for zl_ in (0, 1):
            normalize(y2, zl_, p, xr[p, slot(y2, zl_), :])
        ag(10, p).start()

    def stage_product(p):
        for kind in (7, 8, 9, 10):
            ag_wait(kind, p)
        chosen = own_rows(p)
        for f in range(2):
            pbuf[p, :, part(f)] = dot(xg[p], w[:, part(f)]).astype(bf16)
            first(0, f, p).start()
            first(1, f, p).start()
        for f in range(2):
            second(0, 0, f, p).start()
            second(1, 1, f, p).start()
        for f in range(2):
            own = jnp.concatenate([pbuf[p, half(0, d), part(f)], pbuf[p, half(1, d), part(f)]], axis=0)
            wout[p, :, part(f)] = (own.astype(f32) + (bias[:, part(f)] - dot(chosen, sent[:, part(f)]))).astype(bf16)
            base(f, p).start()

    def stage_sum(p):
        for f in range(2):
            for way in (0, 1):
                first(way, f, p).wait_recv()
                rows = half(1 - way, dn if way == 0 else dq)
                pbuf[p, rows, part(f)] = (
                    pbuf[p, rows, part(f)].astype(f32) + m1[p, way, :, part(f)].astype(f32)
                ).astype(bf16)
                second(way, 1 - way, f, p).start()

    def stage_code(p):
        chosen = own_rows(p)
        rows = pl.ds(pl.multiple_of(p * PR, PR), PR)
        for f in range(2):
            base(f, p).wait_recv()
            for way in (0, 1):
                for h in (0, 1):
                    second(way, h, f, p).wait_recv()
            for b in range(PARTS[f][1] // HB):
                columns = pl.ds(PARTS[f][0] + b * HB, HB)
                other = [m2[p, 0, h, :, columns].astype(f32) + m2[p, 1, h, :, columns].astype(f32) for h in (0, 1)]
                delta = win[p, :, columns].astype(f32) + jnp.concatenate(other, axis=0)
                high = delta.astype(bf16)
                low = (delta - high.astype(f32)).astype(bf16)
                coded = clipped(dot(jnp.concatenate([high, low], axis=1), table[0 : 2 * HB]))
                value = dot(
                    jnp.concatenate([chosen, coded], axis=1),
                    jnp.concatenate([held[:, columns], table[0:HB]], axis=0),
                ).astype(bf16)
                for i, q in enumerate((0, 2, 1, 3)):
                    obuf[q, rows, columns] = value[i * PR : (i + 1) * PR]

    def stage_grad(g):
        for b in range(GB):
            columns = pl.ds(pl.multiple_of(g * GC + b * HB, HB), HB)
            stored = dot(ohg[...], bs[:, columns]).astype(bf16)
            tu = dot(jnp.concatenate([gi[:, columns], stored], axis=1), table[HB : 3 * HB])
            gwout[g, :, b * HB : (b + 1) * HB] = clipped(tu)
        grad_wire(g).start()

    def stage_grad_decode(g):
        grad_wire(g).wait_recv()
        for b in range(GB):
            columns = pl.ds(pl.multiple_of(g * GC + b * HB, HB), HB)
            gobuf[:, columns] = dot(
                jnp.concatenate([ohg[...], gwin[g, :, b * HB : (b + 1) * HB]], axis=1),
                jnp.concatenate([bh[:, columns], table[0:HB]], axis=0),
            ).astype(bf16)

    def stage_finish(p):
        for kind in range(11):
            ag(kind, p).wait_send()
        for f in range(2):
            for way in (0, 1):
                first(way, f, p).wait_send()
                for h in (0, 1):
                    second(way, h, f, p).wait_send()
            base(f, p).wait_send()

    def stage_finish_grad(g):
        grad_wire(g).wait_send()

    def at(k, delay, stage, count=PIECES):
        p = k - delay

        @pl.when((p >= 0) & (p < count))
        def _():
            stage(p)

    def tick(k, carry):
        at(k, 2, stage_opposite)
        at(k, 1, stage_far)
        at(k, 0, stage_near)
        at(k, -AHEAD, stage_next)

        @pl.when(k == 0)
        def _():
            stats_total()
            lax.fori_loop(AHEAD, PIECES, own, 0)

        @pl.when(k == 1)
        def _():
            stats_come()

        at(k, 1, stage_normalize)

        @pl.when(k == 2)
        def _():
            for load in loads[8:]:
                load.wait()

        at(k, 2, stage_product)
        at(k, GRAD_DELAY, stage_grad, GSTEPS)
        at(k, GRAD_DELAY + 2, stage_grad_decode, GSTEPS)
        at(k, GRAD_DELAY + 3, stage_finish_grad, GSTEPS)
        at(k, 3, stage_sum)
        at(k, CODE_DELAY, stage_code)
        at(k, CODE_DELAY, stage_finish, PIECES - 1)
        return carry

    def own(p, carry):
        stage_own(p)
        return carry

    pl.semaphore_wait(barrier, len(peers))
    for p in range(AHEAD):
        stage_own(p)
        stage_next(p)
    loads[0].wait()
    stats_send()
    for load in loads[6:]:
        load.start()
    for load in loads[1:6]:
        load.wait()
    for q in range(4):
        oha[q] = picked(aids[q : q + 1, :])
    ohg[...] = picked(gids[0:1, :])
    loads[6].wait()
    loads[7].wait()
    lax.fori_loop(0, PIECES + CODE_DELAY, tick, 0)
    for j in range(7):
        tok_copy(j).wait_send()
    for j in range(3):
        st_copy(j).wait_send()

    stage_finish(PIECES - 1)


def shards(
    act_input, ln_gain, ln_shift, w_proj, b_proj, act_ids, sent_copy, held_copy,
    grad_input, grad_ids, back_sent, back_held,
):
    anywhere = pl.BlockSpec(memory_space=pl.ANY)
    vmem = pl.BlockSpec(memory_space=pltpu.VMEM)
    dma = pltpu.SemaphoreType.DMA
    arrived, grad_arrived = pl.pallas_call(
        kernel,
        out_shape=(
            pltpu.VMEM((4, TR, ND), bf16),
            pltpu.VMEM((TR, KD), bf16),
        ),
        in_specs=[anywhere] * 12,
        out_specs=(vmem, vmem),
        scratch_shapes=[
            pltpu.VMEM((TR, KD), bf16),
            pltpu.VMEM((1, KD), f32),
            pltpu.VMEM((1, KD), f32),
            pltpu.VMEM((1, ND), f32),
            pltpu.VMEM((4, TR), jnp.int32),
            pltpu.VMEM((1, TR), jnp.int32),
            pltpu.VMEM((KD, ND), bf16),
            pltpu.VMEM((HB, ND), bf16),
            pltpu.VMEM((HB, ND), bf16),
            pltpu.VMEM((TR, KD), bf16),
            pltpu.VMEM((HB, KD), bf16),
            pltpu.VMEM((HB, KD), bf16),
            pltpu.VMEM((PIECES, PLANE, KD), bf16),
            pltpu.VMEM((PIECES, 2 * PLANE, KD), bf16),
            pltpu.VMEM((PIECES, 2 * PLANE, ND), bf16),
            pltpu.VMEM((PIECES, 2, 2 * PR, ND), bf16),
            pltpu.VMEM((PIECES, 2, 2, 2 * PR, ND), bf16),
            pltpu.VMEM((PIECES, 4 * PR, ND), bf16),
            pltpu.VMEM((PIECES, 4 * PR, ND), bf16),
            pltpu.VMEM((GSTEPS, TR, GC), bf16),
            pltpu.VMEM((GSTEPS, TR, GC), bf16),
            pltpu.VMEM((3 * HB, HB), bf16),
            pltpu.VMEM((4, TR, HB), bf16),
            pltpu.VMEM((TR, HB), bf16),
            pltpu.VMEM((8, HB), f32),
            pltpu.VMEM((3, 8, HB), f32),
            pltpu.VMEM((8, HB), f32),
            pltpu.VMEM((7, 8, HB), f32),
            pltpu.VMEM((8, TR, HB), f32),
            dma((12,)),
            dma((PIECES, 11)),
            dma((PIECES, 11)),
            dma((PIECES, 2, 2)),
            dma((PIECES, 2, 2)),
            dma((PIECES, 2, 2, 2)),
            dma((PIECES, 2, 2, 2)),
            dma((PIECES, 2)),
            dma((PIECES, 2)),
            dma((GSTEPS,)),
            dma((GSTEPS,)),
            dma((3,)),
            dma((3,)),
            dma((7,)),
            dma((7,)),
        ],
        compiler_params=pltpu.CompilerParams(
            collective_id=0, has_side_effects=True, vmem_limit_bytes=56 * 2**20
        ),
        cost_estimate=pl.CostEstimate(
            flops=2 * 2048 * KD * ND, bytes_accessed=14 * 2**20, transcendentals=0
        ),
        name="relay",
    )(
        act_input[0], ln_gain, ln_shift, w_proj[0], b_proj, act_ids.reshape(4, TR),
        sent_copy[0], held_copy[0], grad_input[0], grad_ids.reshape(1, TR), back_sent[0], back_held[0],
    )
    return (arrived.reshape(1, 4 * TR, ND), grad_arrived[None])


def solution(mesh):
    placed = (
        P("section", "tensor", "dp"),
        P("section", "dp"),
        P("section", "dp"),
        P("section", "dp", "tensor"),
        P("section", "tensor"),
        P("dp"),
        P("section", "dp", "tensor"),
        P("section", "dp", "tensor"),
        P("section", "tensor", "dp"),
        P("tensor"),
        P("section", "tensor", "dp"),
        P("section", "tensor", "dp"),
    )
    return jax.shard_map(
        shards,
        mesh=mesh,
        in_specs=placed,
        out_specs=(P("section", "dp", "tensor"), P("section", "tensor", "dp")),
        check_vma=False,
    )
```
